256 devices in a mesh: seg: 8 (over z_lo, x), term: 16 (over z_hi, y), sec: 2 (over core).
Axes of the slice: x: 4, y: 4, z: 8 (z_hi: 4, z_lo: 2; z = z_hi * 2 + z_lo), core: 2. Of those that a mesh axis runs over, the one named last changes fastest.
Arguments:
- wavefunction: bfloat16 [8, 16, 16, 128, 128], P('seg', None, 'sec'), may hold values from -6 to 6
- left_env: bfloat16 [8, 64, 16, 128, 128], P('seg', 'term', 'sec'), may hold values from -6 to 6
- right_env: bfloat16 [8, 64, 16, 128, 128], P('seg', 'term', 'sec'), may hold values from -0.5 to 0.5
- mpo_mix: bfloat16 [64, 16, 16], replicated, may hold values from -0.1875 to 0.1875
- env_weight: float32 [64, 16], P('term'), may hold values from -1.5 to 1.5
- env_mix: float32 [64, 64], P(None, 'term'), may hold values from -0.75 to 0.75
- term_shift: int32 [64], replicated, may hold values from -1 to 1
- sector_dims: int32 [16], P('sec'), may hold values from 64 to 128, as said below
Outputs:
- applied: bfloat16 [8, 16, 16, 128, 128], P('seg', 'term', 'sec')
- new_env: bfloat16 [8, 64, 16, 128, 128], P('seg', 'term', 'sec')
The draws below stay inside these ranges and needn't reach their ends.
Inputs may be any that keep to these rules, and one draw needn't show every extreme that they name: sector_dims gives the live states of each sector; padded rows and columns of every block are masked; some sector has 128 and some 128 // 2. Each term moves the sector by term_shift, cyclically over 16 sectors.
All inputs are finite; a program needn't handle non-finite values.
Results may differ from the reference program's by a relative error of at most 0.0074.
Values may be sent and summed in bfloat16 or wider, within the bound.
No kernel may reach another device: no remote copies, remote signals or barrier semaphores. Data moves between devices by JAX's collectives and lax.ppermute only.
A program may use at most 128 MiB of HBM per device.

```python
import jax
import jax.numpy as jnp
from jax import lax

BLK = 128
NSEC = 16
P_SIZE = 16
W = 64
SEGS = 8


def draw_sector_dims(key, part):
    key = jax.random.fold_in(key, 7)
    key_dims, key_top, key_low = jax.random.split(key, 3)
    dims = jax.random.randint(key_dims, (NSEC,), BLK // 2, BLK + 1)
    top_index = jax.random.randint(key_top, (), 0, NSEC)
    low_index = (top_index + 1 + jax.random.randint(key_low, (), 0, NSEC - 1)) % NSEC
    dims = dims.at[top_index].set(BLK)
    dims = dims.at[low_index].set(BLK // 2)
    return dims.astype(jnp.int32)


def plant(entries, rng, smallest, largest):
    longest = entries.shape.index(max(entries.shape))
    spots = []
    for shift in (0, 1):
        where = [jax.random.randint(jax.random.fold_in(rng, axis), (), 0, length) for axis, length in enumerate(entries.shape)]
        where[longest] = (where[longest] + shift) % entries.shape[longest]
        spots.append(tuple(where))
    return entries.at[spots[0]].set(smallest).at[spots[1]].set(largest)


def level_of(stream_key, extent, cuts, least, top_value):
    gain = 1.0
    for position, shards_of in cuts:
        steps = jax.random.uniform(jax.random.fold_in(jax.random.fold_in(stream_key, 6), position), (shards_of,), jnp.float32, least / len(cuts), top_value / len(cuts))
        gain = gain * jnp.repeat(jnp.exp(steps), extent[position] // shards_of).reshape((-1,) + (1,) * (len(extent) - 1 - position))
    return gain


def noise(stream_key, extent, width, bound, cuts=(), kind=jnp.bfloat16):
    result = width * jax.random.normal(stream_key, extent, jnp.float32)
    if cuts:
        result = result * level_of(stream_key, extent, cuts, -0.22, 0.18)
    return jnp.clip(result, -bound, bound).astype(kind)


def setup_inputs(seed: int = 0) -> dict:
    splits = jax.random.split(jax.random.key(seed), 9)
    wavefunction = noise(splits[0], (SEGS, P_SIZE, NSEC, BLK, BLK), 1.0, 6.0, ((0, 8), (2, 2)))
    left_env = noise(splits[1], (SEGS, W, NSEC, BLK, BLK), 1.0, 6.0, ((0, 8), (1, 16), (2, 2)))
    right_env = noise(splits[2], (SEGS, W, NSEC, BLK, BLK), BLK ** -0.5, 0.5, ((0, 8), (1, 16), (2, 2)))
    mpo_mix = noise(splits[3], (W, P_SIZE, P_SIZE), (W * P_SIZE) ** -0.5, 0.1875)
    env_weight = noise(splits[4], (W, P_SIZE), P_SIZE ** -0.5, 1.5, ((0, 16),), jnp.float32)
    env_mix = noise(splits[5], (W, W), W ** -0.5, 0.75, ((1, 16),), jnp.float32)
    term_shift = plant(jax.random.randint(splits[6], (W,), -1, 2), jax.random.fold_in(splits[6], 1), -1, 1).astype(jnp.int32)
    sector_dims = draw_sector_dims(jax.random.fold_in(splits[8], 71), 0)
    return {"wavefunction": wavefunction, "left_env": left_env, "right_env": right_env, "mpo_mix": mpo_mix, "env_weight": env_weight, "env_mix": env_mix, "term_shift": term_shift, "sector_dims": sector_dims}


def live_pair(sector_dims):
    live_rows = jnp.arange(BLK)[None, :] < sector_dims[:, None]
    return live_rows[:, :, None] & live_rows[:, None, :]


def reference(wavefunction, left_env, right_env, mpo_mix, env_weight, env_mix, term_shift, sector_dims):
    highest = lax.Precision.HIGHEST
    pair = live_pair(sector_dims)
    field = jnp.where(pair[None, None], wavefunction, jnp.zeros((), wavefunction.dtype))
    term_ids = jnp.arange(W).astype(jnp.int32)
    env_list = []
    for segment in range(SEGS):
        part = field[segment].astype(jnp.float32)

        def env_term(w_index):
            lpsi = jnp.einsum('kab,pkbc->pkac', left_env[segment, w_index].astype(jnp.float32), part, precision=highest)
            weighted = (lpsi * (env_weight[w_index] / BLK)[:, None, None, None]).astype(jnp.bfloat16)
            return jnp.einsum('pkba,pkbc->kac', part, weighted.astype(jnp.float32), precision=highest).astype(jnp.bfloat16)

        env_part = lax.map(env_term, term_ids)
        mixed_env = jnp.einsum('wv,wkab->vkab', env_mix, env_part.astype(jnp.float32), precision=highest)
        env_list.append(mixed_env.astype(jnp.bfloat16))
    new_env = jnp.stack(env_list)
    left_used = jnp.concatenate([left_env[:1], new_env[:-1]], axis=0)
    applied_list = []
    for segment in range(SEGS):
        part = field[segment].astype(jnp.float32)

        def term_step(total, w_index):
            shifted = jnp.roll(part, -term_shift[w_index], axis=1)
            mixed = jnp.einsum('qp,pkab->qkab', mpo_mix[w_index].astype(jnp.float32), shifted, precision=highest).astype(jnp.bfloat16)
            right_part = jnp.einsum('qkab,kcb->qkac', mixed.astype(jnp.float32), right_env[segment, w_index].astype(jnp.float32), precision=highest).astype(jnp.bfloat16)
            added = jnp.einsum('kab,qkbc->qkac', left_used[segment, w_index].astype(jnp.float32), right_part.astype(jnp.float32), precision=highest)
            return total + added, None

        total, unused = lax.scan(term_step, jnp.zeros((P_SIZE, NSEC, BLK, BLK), jnp.float32), term_ids)
        scaled = jnp.where(pair[None], total * (BLK ** -0.5), jnp.zeros((), jnp.float32))
        applied_list.append(scaled.astype(jnp.bfloat16))
    return jnp.stack(applied_list), new_env
```

```python
import functools

import jax
import jax.numpy as jnp
from jax import lax
from jax.experimental import pallas as pl
from jax.experimental.pallas import tpu as pltpu
from jax.sharding import PartitionSpec as P

BF16 = jnp.bfloat16
F32 = jnp.float32
ROWS = 16
SIDE = 4
CHUNKS = 4
VMEM_LIMIT = 48 * 1024 * 1024


def call(body, *, grid, in_specs, out_specs, out_shape, scratch=(), prefetch=0, flops=0, moved=0):
    return pl.pallas_call(
        body,
        grid_spec=pltpu.PrefetchScalarGridSpec(
            num_scalar_prefetch=prefetch,
            grid=grid,
            in_specs=in_specs,
            out_specs=out_specs,
            scratch_shapes=scratch,
        ),
        out_shape=out_shape,
        compiler_params=pltpu.CompilerParams(vmem_limit_bytes=VMEM_LIMIT),
        cost_estimate=pl.CostEstimate(flops=flops, bytes_accessed=moved, transcendentals=0),
    )


def blocks_spec(count, block, first):
    return pl.BlockSpec((count, 1, block, block), lambda k, *_: (0, first + k, 0, 0))


def whole(shape):
    return pl.BlockSpec(shape, lambda *_: (0,) * len(shape))


SCALARS = pl.BlockSpec(memory_space=pltpu.SMEM)


def live_block(size, block):
    rows = lax.broadcasted_iota(jnp.int32, (block, block), 0)
    cols = lax.broadcasted_iota(jnp.int32, (block, block), 1)
    return jnp.where((rows < size) & (cols < size), 1.0, 0.0)


def env_body(first, dims, weight, wave, left, out, field, weighted):
    block = wave.shape[-1]
    pairs, terms = wave.shape[0], left.shape[0]
    live = live_block(dims[first + pl.program_id(0)], block).astype(BF16)
    stacked = left[:, 0].reshape(terms * block, block)
    for p in range(pairs):
        cells = wave[p, 0] * live
        field[p * block : (p + 1) * block, :] = cells
        product = jnp.dot(stacked, cells, preferred_element_type=F32)
        for w in range(terms):
            scaled = product[w * block : (w + 1) * block] * (weight[w, p] * (1.0 / block))
            weighted[p * block : (p + 1) * block, w * block : (w + 1) * block] = scaled.astype(BF16)
    total = lax.dot_general(
        field[...], weighted[...], (((0,), (0,)), ((), ())), preferred_element_type=F32
    )
    for w in range(terms):
        out[w, 0] = total[:, w * block : (w + 1) * block].astype(BF16)


def env_chunk(dims, weight, wave, left, first, count):
    pairs, _, block, _ = wave.shape
    terms = left.shape[0]
    return call(
        functools.partial(env_body, first),
        grid=(count,),
        in_specs=[SCALARS, SCALARS, blocks_spec(pairs, block, first), blocks_spec(terms, block, first)],
        out_specs=blocks_spec(terms, block, 0),
        out_shape=jax.ShapeDtypeStruct((terms, count, block, block), BF16),
        scratch=[
            pltpu.VMEM((pairs * block, block), BF16),
            pltpu.VMEM((pairs * block, terms * block), BF16),
        ],
        flops=4 * count * pairs * terms * block**3,
        moved=2 * count * (pairs + 2 * terms) * block**2,
    )(dims, weight, wave, left)


def by_rows(groups, block):
    return jnp.concatenate(
        [
            jnp.concatenate([g[:, 0, r : r + ROWS, :] for g in groups], axis=0).reshape(-1, block)
            for r in range(0, block, ROWS)
        ],
        axis=1,
    )


def mix_body(kron, e0, e1, e2, e3, *outs):
    block = e0.shape[-1]
    cells = by_rows([e0, e1, e2, e3], block)
    both = jnp.dot(kron[...], cells, preferred_element_type=F32)
    half = both.shape[0] // 2
    mixed = both[:half] + both[half:]
    share = half // SIDE
    for d, out in enumerate(outs):
        for i, r in enumerate(range(0, block, ROWS)):
            part = mixed[d * share : (d + 1) * share, i * block : (i + 1) * block]
            out[:, 0, r : r + ROWS, :] = part.reshape(-1, ROWS, block).astype(out.dtype)


def mix_chunk(kron, parts, dtypes):
    terms, count, block, _ = parts[0].shape
    return call(
        mix_body,
        grid=(count,),
        in_specs=[whole(kron.shape)] + [blocks_spec(terms, block, 0)] * SIDE,
        out_specs=[blocks_spec(terms, block, 0)] * SIDE,
        out_shape=[jax.ShapeDtypeStruct(parts[0].shape, t) for t in dtypes],
        flops=4 * count * 256 * 256 * block * (block // ROWS),
        moved=10 * count * 16 * block**2,
    )(kron, *parts)


def right_body(terms, shift, kron, *refs):
    fields, right, out, mixed = refs[:terms], refs[terms], refs[terms + 1], refs[terms + 2]
    block = right.shape[-1]
    pairs = mixed.shape[0]
    for w in range(terms):
        cells = by_rows([fields[w]], block)
        sums = jnp.dot(kron[w], cells, preferred_element_type=F32).astype(BF16)
        for i, r in enumerate(range(0, block, ROWS)):
            mixed[:, r : r + ROWS, :] = sums[:, i * block : (i + 1) * block].reshape(-1, ROWS, block)
        part = lax.dot_general(
            mixed[...].reshape(pairs * block, block),
            right[w, 0],
            (((1,), (1,)), ((), ())),
            preferred_element_type=F32,
        ).astype(BF16)
        for q in range(pairs):
            out[0, w * block : (w + 1) * block, q * block : (q + 1) * block] = part[
                q * block : (q + 1) * block
            ]


def right_chunk(shift, kron, padded, right, first, count):
    pairs, _, block, _ = padded.shape
    terms = right.shape[0]

    def field_spec(w):
        return pl.BlockSpec(
            (pairs, 1, block, block), lambda k, s: (0, first + 1 + k + s[w], 0, 0)
        )

    return call(
        functools.partial(right_body, terms),
        grid=(count,),
        prefetch=1,
        in_specs=[whole(kron.shape)]
        + [field_spec(w) for w in range(terms)]
        + [blocks_spec(terms, block, first)],
        out_specs=pl.BlockSpec((1, terms * block, pairs * block), lambda k, s: (k, 0, 0)),
        out_shape=jax.ShapeDtypeStruct((count, terms * block, pairs * block), BF16),
        scratch=[pltpu.VMEM((pairs, block, block), BF16)],
        flops=2 * count * terms * pairs * block**2 * (block + 256),
        moved=2 * count * terms * (2 * pairs + 1) * block**2,
    )(shift, kron, *([padded] * terms), right)


def left_body(seg, left, received, right_part, *refs):
    outs, used = refs[:-1], refs[-1]
    block = left.shape[-1]
    terms = left.shape[0]

    @pl.when(seg[0] == 0)
    def _():
        for w in range(terms):
            used[:, w * block : (w + 1) * block] = left[w, 0]

    @pl.when(seg[0] != 0)
    def _():
        for w in range(terms):
            used[:, w * block : (w + 1) * block] = received[w, 0]

    width = SIDE * block
    for d, out in enumerate(outs):
        total = jnp.dot(
            used[...], right_part[0, :, d * width : (d + 1) * width], preferred_element_type=F32
        )
        for e in range(SIDE):
            out[e, 0] = total[:, e * block : (e + 1) * block].astype(out.dtype)


def left_chunk(seg, left, received, right_part, first, dtypes):
    terms, count, block, _ = received.shape
    shape = (SIDE, count, block, block)
    return call(
        left_body,
        grid=(count,),
        in_specs=[
            SCALARS,
            blocks_spec(terms, block, first),
            blocks_spec(terms, block, 0),
            pl.BlockSpec((1,) + right_part.shape[1:], lambda k: (k, 0, 0)),
        ],
        out_specs=[blocks_spec(SIDE, block, 0)] * SIDE,
        out_shape=[jax.ShapeDtypeStruct(shape, t) for t in dtypes],
        scratch=[pltpu.VMEM((block, terms * block), BF16)],
        flops=2 * count * terms * SIDE * SIDE * block**3,
        moved=2 * count * (terms * 18 + 16) * block**2,
    )(seg, left, received, right_part)


def collect_body(own, one, two, *outs):
    for e, out in enumerate(outs):
        total = own[e, 0] + one[e, 0].astype(F32) + two[e, 0].astype(F32)
        out[0, 0] = total.astype(out.dtype)


def collect_chunk(own, one, two, dtypes):
    _, count, block, _ = own.shape
    return call(
        collect_body,
        grid=(count,),
        in_specs=[blocks_spec(SIDE, block, 0)] * 3,
        out_specs=[blocks_spec(1, block, 0)] * SIDE,
        out_shape=[jax.ShapeDtypeStruct((1, count, block, block), t) for t in dtypes],
        flops=0,
        moved=12 * count * SIDE * block**2,
    )(own, one, two)


def along(step, dim):
    def target(i):
        z, y = i // SIDE, i % SIDE
        if dim == "z":
            return (z + step) % SIDE * SIDE + y
        return z * SIDE + (y + step) % SIDE

    return [(i, target(i)) for i in range(SIDE * SIDE)]


def sent(cells, step, dim):
    return lax.ppermute(cells, "term", along(step, dim))


def near(step):
    return step % SIDE


def gathered(own, way):
    ahead = sent(own, 1, "z")
    back = sent(own, -1, "z")
    far = sent(ahead if way > 0 else back, way, "z")
    return own, back, far, ahead


def part_types(way):
    types = [F32, BF16, BF16, BF16]
    types[near(way)] = F32
    return types


def reduced(parts, way, dim):
    far = sent(parts[2], way, dim)
    direct = sent(parts[near(-way)], -way, dim)
    joined = (parts[near(way)] + far.astype(F32)).astype(BF16)
    return direct, sent(joined, way, dim)


def spread(coefficients):
    count = coefficients.shape[-1]
    size = count * ROWS
    rows = jnp.arange(size)
    pick = (rows[:, None] // ROWS == jnp.arange(count)[None, :]).astype(F32)
    same = rows[:, None] % ROWS == rows[None, :] % ROWS
    full = jnp.einsum(
        "rq,...qp,sp->...rs", pick, coefficients.astype(F32), pick, precision=lax.Precision.HIGHEST
    )
    return jnp.where(same, full, 0.0)


def rolled(cells, start, axis):
    size = cells.shape[axis]
    return lax.dynamic_slice_in_dim(jnp.concatenate([cells, cells], axis), start, size, axis)


def per_device(
    wavefunction, left_env, right_env, mpo_mix, env_weight, env_mix, term_shift, sector_dims
):
    wave, left, right = wavefunction[0], left_env[0], right_env[0]
    pairs, sectors, block, _ = wave.shape
    terms = left.shape[0]
    me = lax.axis_index("term")
    my_z, my_y = me // SIDE, me % SIDE
    seg = lax.axis_index("seg").astype(jnp.int32).reshape(1)
    live_rows = jnp.arange(block)[None, :] < sector_dims[:, None]
    live = live_rows[:, :, None] & live_rows[:, None, :]
    masked = jnp.where(live[None], wave, jnp.zeros((), BF16))
    edges = jnp.concatenate([masked[:, :1], masked[:, -1:]], axis=1)
    swapped = lax.ppermute(edges, "sec", [(0, 1), (1, 0)])
    padded = jnp.concatenate([swapped[:, 1:], masked, swapped[:, :1]], axis=1)

    mpo_local = lax.dynamic_slice_in_dim(mpo_mix, me * terms, terms, 0)
    mpo_local = mpo_local.reshape(terms, SIDE, SIDE, pairs)
    mpo_local = rolled(rolled(mpo_local, my_z, 1), my_y, 2)
    mpo_local = mpo_local.transpose(0, 2, 1, 3).reshape(terms, pairs, pairs)
    mpo_kron = spread(mpo_local).astype(BF16)
    shift = lax.dynamic_slice_in_dim(term_shift, me * terms, terms, 0)

    columns = jnp.stack([env_mix] + [sent(env_mix, -d, "y") for d in range(1, SIDE)])
    columns = columns.reshape(SIDE, SIDE, SIDE, terms, terms)
    columns = lax.dynamic_index_in_dim(columns, my_y, 2, keepdims=False)
    columns = rolled(columns, my_z, 1)
    columns = columns.transpose(0, 3, 1, 2).reshape(SIDE * terms, SIDE * terms)
    env_full = spread(columns)
    env_high = lax.reduce_precision(env_full, 8, 7)
    env_kron = jnp.concatenate([env_high, env_full - env_high], axis=0).astype(BF16)

    count = sectors // CHUNKS
    new_parts, out_parts = [], []
    for c in range(CHUNKS):
        first = c * count
        way = 1 if c % 2 == 0 else -1
        own = env_chunk(sector_dims, env_weight, wave, left, first, count)
        mixed = mix_chunk(env_kron, gathered(own, way), part_types(way))
        one, two = reduced(mixed, way, "y")
        new = (mixed[0] + one.astype(F32) + two.astype(F32)).astype(BF16)
        new_parts.append(new)
        segments = lax.axis_size("seg")
        received = lax.ppermute(new, "seg", [(i, i + 1) for i in range(segments - 1)])
        right_part = right_chunk(shift, mpo_kron, padded, right, first, count)
        sums = left_chunk(seg, left, received, right_part, first, part_types(way))
        one, two = reduced(sums, way, "y")
        shares = collect_chunk(sums[0], one, two, part_types(way))
        one, two = reduced(shares, way, "z")
        total = shares[0] + one.astype(F32) + two.astype(F32)
        scaled = jnp.where(live[None, first : first + count], total * block**-0.5, 0.0)
        out_parts.append(scaled.astype(BF16))
    applied = jnp.concatenate(out_parts, axis=1)
    new_env = jnp.concatenate(new_parts, axis=1)
    return applied[None], new_env[None]


def solution(mesh):
    return jax.shard_map(
        per_device,
        mesh=mesh,
        in_specs=(
            P("seg", None, "sec", None, None),
            P("seg", "term", "sec", None, None),
            P("seg", "term", "sec", None, None),
            P(),
            P("term", None),
            P(None, "term"),
            P(),
            P("sec"),
        ),
        out_specs=(P("seg", "term", "sec", None, None), P("seg", "term", "sec", None, None)),
        check_vma=False,
    )
```
